1024 devices in a mesh: dp: 16 (over z_hi, x), pipe: 16 (over y, core), mp: 4 (over z_lo).
Axes of the slice: x: 4, y: 8, z: 16 (z_hi: 4, z_lo: 4; z = z_hi * 4 + z_lo), core: 2. Of those that a mesh axis runs over, the one named last changes fastest.
Arguments:
- stash: bfloat16 [16, 16, 10, 64, 8192], P('pipe', 'dp', None, None, 'mp')
- own_input: bfloat16 [16, 16, 128, 8192], P('pipe', 'dp', None, 'mp')
- gain: bfloat16 [16, 8192], P('pipe', 'mp'), may hold values from 0.099609375 to 1.8984375
- key_weight: bfloat16 [16, 8192, 512], P('pipe', 'mp'), may hold values from -0.0625 to 0.0625
- own_cotangent: bfloat16 [16, 16, 128, 512], P('pipe', 'dp'), may hold values from -0.3125 to 0.3125
- replay_cotangent: bfloat16 [16, 16, 2, 64, 512], P('pipe', 'dp'), may hold values from -0.3125 to 0.3125
- failed: int32 [16], replicated, may hold values from 0 to 15
- counts: int32 [16, 16], replicated, may hold values from 0 to 2, as said below
- table: int32 [16, 16, 2], replicated, may hold values from 0 to 9, as said below
Outputs:
- replayed_keys: bfloat16 [16, 16, 2, 64, 512], P('pipe', 'dp', None, None, 'mp')
- weight_grad: float32 [16, 8192, 512], P('pipe', ('mp', 'dp'))
The draws below stay inside these ranges and needn't reach their ends.
Inputs may be any that keep to these rules, and one draw needn't show every extreme that they name: Per section the counts sum to 10; the failed replica's count is 0; some replica of every section has exactly 2. `table`: per section, the first counts[s, r] entries of the replicas' rows name each of the 10 microbatches exactly once; later entries are arbitrary and unused.
All inputs are finite; a program needn't handle non-finite values.
Results may differ from the reference program's by a relative error of at most 0.02.
Values may be sent and summed in bfloat16 or wider, within the bound.
A program may use at most 32 MiB of HBM per device.

```python
import math
import jax
import jax.numpy as jnp
from jax import lax

D = 8192
KV = 512
TOK = 64
MB = 10
MOST = 2
OWN = 128
PIPE = 16
DP = 16


def routing(key):
    key_fail, key_order, key_slots, key_batch, key_spare, key_dead, key_section = jax.random.split(key, 7)
    failed_rows = jax.random.randint(key_fail, (PIPE,), 0, DP, dtype=jnp.int32)
    section_order = jax.random.permutation(key_section, jnp.arange(PIPE, dtype=jnp.int32))
    failed_rows = failed_rows.at[section_order[0]].set(DP - 1)
    failed_rows = failed_rows.at[section_order[1]].set(0)
    offsets = jax.vmap(lambda one_key: jax.random.permutation(one_key, jnp.arange(1, DP, dtype=jnp.int32)))(jax.random.split(key_order, PIPE))
    peers = (failed_rows[:, None] + offsets) % DP
    spare_total = (DP - 2) * MOST
    slot_order = jax.vmap(lambda one_key: jax.random.permutation(one_key, jnp.arange(spare_total, dtype=jnp.int32)))(jax.random.split(key_slots, PIPE))
    chosen = slot_order[:, :MB - MOST]
    owners = chosen // MOST
    rest_counts = jnp.sum((owners[:, :, None] == jnp.arange(DP - 2, dtype=jnp.int32)[None, None, :]).astype(jnp.int32), axis=1)
    per_position = jnp.concatenate([jnp.full((PIPE, 1), MOST, jnp.int32), rest_counts.astype(jnp.int32)], axis=1)
    starts = jnp.cumsum(per_position, axis=1) - per_position
    batches = jax.vmap(lambda one_key: jax.random.permutation(one_key, jnp.arange(MB, dtype=jnp.int32)))(jax.random.split(key_batch, PIPE))
    slot_ids = jnp.arange(MOST, dtype=jnp.int32)
    wanted = jnp.clip(starts[:, :, None] + slot_ids[None, None, :], 0, MB - 1).reshape(PIPE, (DP - 1) * MOST)
    picks = jnp.take_along_axis(batches, wanted, axis=1).reshape(PIPE, DP - 1, MOST)
    spare = jax.random.randint(key_spare, (PIPE, DP - 1, MOST), 0, MB, dtype=jnp.int32)
    entries = jnp.where(slot_ids[None, None, :] < per_position[:, :, None], picks, spare)
    section_ids = jnp.arange(PIPE, dtype=jnp.int32)[:, None]
    count_rows = jnp.zeros((PIPE, DP), jnp.int32).at[section_ids, peers].set(per_position)
    table_rows = jax.random.randint(key_dead, (PIPE, DP, MOST), 0, MB, dtype=jnp.int32)
    table_rows = table_rows.at[section_ids, peers].set(entries)
    return (failed_rows, count_rows, table_rows)


def scaled(key, base, row_top):
    key_rows, key_cols = jax.random.split(key, 2)
    ramp = jnp.arange(D, dtype=jnp.float32) / (D - 1)
    columns = jnp.exp(math.log(3.0) * ramp + jax.random.uniform(key_cols, (D,), jnp.float32) * math.log(4.0))
    rows = jnp.exp(jax.random.uniform(key_rows, base.shape[:-1] + (1,), jnp.float32) * math.log(row_top))
    return base * rows * columns


def draw_failed(key, part):
    return routing(key)[0]


def draw_counts(key, part):
    return routing(key)[1]


def draw_table(key, part):
    return routing(key)[2]


def draw_stash(key, part):
    key = jax.random.fold_in(key, 11)
    key_base, key_scale = jax.random.split(key, 2)
    shape = (PIPE, DP, MB, TOK, D)
    base = jax.random.normal(key_base, shape, jnp.float32)
    values = scaled(key_scale, base, 10.0)
    return values.astype(jnp.bfloat16)


def draw_own_input(key, part):
    key = jax.random.fold_in(key, 23)
    key_base, key_scale = jax.random.split(key, 2)
    shape = (PIPE, DP, OWN, D)
    base = jax.random.normal(key_base, shape, jnp.float32)
    values = scaled(key_scale, base, 10.0)
    return values.astype(jnp.bfloat16)


def shard_levels(key, dims, cuts, smallest, high):
    level, own = 1.0, jax.random.fold_in(key, 6)
    for dim, blocks in cuts:
        draws = jnp.exp(jax.random.uniform(jax.random.fold_in(own, dim), (blocks,), jnp.float32, smallest / len(cuts), high / len(cuts)))
        level = level * jnp.repeat(draws, dims[dim] // blocks).reshape([-1 if axis == dim else 1 for axis in range(len(dims))])
    return level


def noise(stream_key, dims, width, reach, cuts=(), kind=jnp.bfloat16):
    values = jax.random.normal(stream_key, dims, jnp.float32) * width
    if len(cuts) > 0:
        values = shard_levels(stream_key, dims, cuts, -0.22, 0.18) * values
    return jnp.clip(values, min=-reach, max=reach).astype(kind)


def setup_inputs(seed: int = 0) -> dict:
    arg_keys = jax.random.split(jax.random.key(seed), 10)
    stash = draw_stash(jax.random.fold_in(arg_keys[9], 71), 0)
    own_input = draw_own_input(jax.random.fold_in(arg_keys[9], 71), 0)
    gain = jnp.clip(1.0 + 0.18 * jax.random.normal(arg_keys[2], (PIPE, D), jnp.float32), 0.099609375, 1.8984375).astype(jnp.bfloat16)
    key_weight = noise(arg_keys[3], (PIPE, D, KV), D ** -0.5, 0.0625, ((0, 16), (1, 4)))
    own_cotangent = noise(arg_keys[4], (PIPE, DP, OWN, KV), 0.02, 0.3125, ((0, 16), (1, 16)))
    replay_cotangent = noise(arg_keys[5], (PIPE, DP, MOST, TOK, KV), 0.02, 0.3125, ((0, 16), (1, 16)))
    failed = draw_failed(jax.random.fold_in(arg_keys[9], 71), 0)
    counts = draw_counts(jax.random.fold_in(arg_keys[9], 71), 0)
    table = draw_table(jax.random.fold_in(arg_keys[9], 71), 0)
    return {"stash": stash, "own_input": own_input, "gain": gain, "key_weight": key_weight, "own_cotangent": own_cotangent, "replay_cotangent": replay_cotangent, "failed": failed, "counts": counts, "table": table}


epsilon = 1e-05

def reference(stash, own_input, gain, key_weight, own_cotangent, replay_cotangent, failed, counts, table):

    def one_section(section_id):
        earlier = (section_id + PIPE - 1) % PIPE
        lost = failed[section_id]
        root_rows = lax.dynamic_index_in_dim(lax.dynamic_index_in_dim(stash, earlier, 0, False), lost, 0, False)
        scaling = lax.dynamic_index_in_dim(gain, section_id, 0, False).astype(jnp.float32)
        weight = lax.dynamic_index_in_dim(key_weight, section_id, 0, False)
        root_float = root_rows.astype(jnp.float32)
        mixed = (root_float * scaling).astype(jnp.bfloat16).reshape(MB * TOK, D)
        factor = lax.rsqrt(lax.optimization_barrier(jnp.sum(root_float * root_float, axis=-1)) / D + epsilon).reshape(MB * TOK)
        keys_batch = (jnp.dot(mixed, weight, preferred_element_type=jnp.float32) * factor[:, None]).astype(jnp.bfloat16)
        keys_batch = keys_batch.reshape(MB, TOK, KV)
        slots = lax.dynamic_index_in_dim(table, section_id, 0, False).astype(jnp.int32)
        numbers = lax.dynamic_index_in_dim(counts, section_id, 0, False)
        live = jnp.arange(MOST, dtype=jnp.int32)[None, :] < numbers[:, None]
        keys_slots = jnp.where(live[:, :, None, None], keys_batch[slots], jnp.zeros((), jnp.bfloat16))
        own_float = lax.dynamic_index_in_dim(own_input, section_id, 0, False).astype(jnp.float32)
        own_mixed = (own_float * scaling).astype(jnp.bfloat16)
        own_factor = lax.rsqrt(lax.optimization_barrier(jnp.sum(own_float * own_float, axis=-1)) / D + epsilon)
        keeper = (jnp.arange(DP, dtype=jnp.int32) != lost).astype(jnp.float32)
        own_cot = lax.dynamic_index_in_dim(own_cotangent, section_id, 0, False).astype(jnp.float32)
        own_back = (own_cot * (own_factor * keeper[:, None])[:, :, None]).astype(jnp.bfloat16)
        factor_batch = factor.reshape(MB, TOK)
        replay_cot = lax.dynamic_index_in_dim(replay_cotangent, section_id, 0, False).astype(jnp.float32)
        replay_back = (replay_cot * factor_batch[slots][:, :, :, None]).astype(jnp.bfloat16)
        mixed_batch = mixed.reshape(MB, TOK, D)

        def add_replica(total, replica):
            contribution = jnp.dot(own_mixed[replica].T, own_back[replica], preferred_element_type=jnp.float32)
            for slot_id in range(MOST):
                batch_id = slots[replica, slot_id]
                piece = lax.cond(live[replica, slot_id], lambda: jnp.dot(mixed_batch[batch_id].T, replay_back[replica, slot_id], preferred_element_type=jnp.float32), lambda: jnp.zeros((D, KV), jnp.float32))
                contribution = contribution + piece
            rounded = lax.optimization_barrier(contribution.astype(jnp.bfloat16)).astype(jnp.float32)
            return (total + rounded, None)
        gradient, _ = lax.scan(add_replica, jnp.zeros((D, KV), jnp.float32), jnp.arange(DP, dtype=jnp.int32))
        return (keys_slots, gradient)
    keys_all, gradients = lax.map(one_section, jnp.arange(PIPE, dtype=jnp.int32))
    return (jnp.roll(keys_all, 1, axis=0), gradients)
```

```python
import functools
import jax
import jax.numpy as jnp
from jax import lax
from jax.experimental import pallas as pl
from jax.experimental.pallas import tpu as pltpu
from jax.sharding import PartitionSpec as P

MESH = pl.DeviceIdType.MESH
XN = 4
ZN = 4
EPS = 1e-05
F32 = jnp.float32
BF16 = jnp.bfloat16


def diagonal(rows, columns):
    return lax.broadcasted_iota(jnp.int32, (rows, columns), 0) == lax.broadcasted_iota(
        jnp.int32, (rows, columns), 1
    )


def to_row(column, columns):
    rows = column.shape[0]
    return jnp.sum(jnp.where(diagonal(rows, columns), column, 0.0), axis=0, keepdims=True)


def to_column(row, rows):
    return jnp.sum(jnp.where(diagonal(rows, row.shape[1]), row, 0.0), axis=1, keepdims=True)


class Copies:
    def __init__(self, send, recv):
        self.send, self.recv, self.count, self.started = send, recv, 0, []

    def start(self, source, target, device):
        copy = pltpu.make_async_remote_copy(
            src_ref=source,
            dst_ref=target,
            send_sem=self.send.at[self.count],
            recv_sem=self.recv.at[self.count],
            device_id=device,
            device_id_type=MESH,
        )
        self.count += 1
        copy.start()
        self.started.append(copy)
        return copy

    def finish(self):
        for copy in self.started:
            copy.wait_send()


def kernel(
    width_total,
    failed,
    counts,
    table,
    stash,
    own_input,
    gain,
    weight,
    own_cotangent,
    replay_cotangent,
    keys_out,
    grad_out,
    cand_p,
    cand_n,
    cand_a,
    cand_b,
    chosen,
    arrived,
    own_in,
    weight_in,
    cot_parts,
    cot_x,
    cot_sum,
    cot_z,
    cot_all,
    own_sum,
    own_sums,
    replay_sum,
    replay_sums,
    mixed,
    back,
    key_parts,
    key_got,
    key_all,
    key_pick,
    key_z,
    key_last,
    key_in,
    grad_parts,
    grad_x,
    grad_half,
    grad_z,
    local_sem,
    send_sem,
    recv_sem,
):
    section = lax.axis_index("pipe")
    replica = lax.axis_index("dp")
    m = lax.axis_index("mp")
    sections = lax.axis_size("pipe")
    widths = lax.axis_size("mp")
    x = lax.rem(replica, XN)
    z = replica // XN
    half, features = stash.shape[1:]
    chunk = 2 * half
    own_rows = own_input.shape[0]
    key_width = weight.shape[1]
    share = key_width // widths
    block = features // (XN * ZN)
    upcoming = lax.rem(section + 1, sections)
    previous = lax.rem(section + sections - 1, sections)

    def x_peer(k):
        return {"dp": z * XN + lax.rem(x + k, XN)}

    def z_peer(k):
        return {"dp": lax.rem(z + k, ZN) * XN + x}

    def m_peer(k):
        return {"mp": lax.rem(m + k, widths)}

    loads = []

    def load(source, target):
        copy = pltpu.make_async_copy(source, target, local_sem.at[len(loads)])
        copy.start()
        loads.append(copy)
        return copy

    load_own = load(own_input, own_in)
    load_p = load(stash.at[2 * lax.rem(x + 1, XN)], cand_p.at[0])
    load_n = load(stash.at[2 * lax.rem(x + 3, XN) + 1], cand_n.at[0])
    load_a = load(stash.at[2 * x], cand_a.at[0])
    load_b = load(stash.at[2 * x + 1], cand_b.at[0])
    load_w = load(weight, weight_in)

    barrier = pltpu.get_barrier_semaphore()
    peers = [x_peer(k) for k in range(1, XN)]
    peers += [z_peer(k) for k in range(1, ZN)]
    peers += [m_peer(k) for k in range(1, widths)]
    peers += [{"pipe": upcoming}, {"pipe": previous}]
    for peer in peers:
        pl.semaphore_signal(barrier, inc=1, device_id=peer, device_id_type=MESH)
    pl.semaphore_wait(barrier, len(peers))

    copies = Copies(send_sem, recv_sem)

    far = 2 * lax.rem(x + 2, XN)
    far_p = copies.start(stash.at[far], cand_p.at[1], x_peer(1))
    far_n = copies.start(stash.at[far + 1], cand_n.at[1], x_peer(3))
    near_b = copies.start(stash.at[2 * lax.rem(x + 1, XN) + 1], cand_b.at[1], x_peer(1))
    near_a = copies.start(stash.at[2 * lax.rem(x + 3, XN)], cand_a.at[1], x_peer(3))

    quarter = pl.ds(pl.multiple_of(m * share, 128), share)
    slot_total = 2
    token_total = replay_cotangent.shape[0] // slot_total
    batches = 4 * chunk // token_total
    live = counts[section, replica]
    cot = replay_cotangent[:, quarter].astype(F32)
    for batch in range(batches):
        value = None
        for j in range(slot_total):
            hit = jnp.logical_and(table[section, 2 * replica + j] == batch, live > j)
            term = cot[j * token_total : (j + 1) * token_total] * hit.astype(F32)
            value = term if value is None else value + term
        cot_parts[batch * token_total : (batch + 1) * token_total] = value.astype(BF16)

    def rows_of(place):
        return pl.ds(pl.multiple_of(place * chunk, 16), chunk)

    cot_copies = [
        copies.start(cot_parts.at[rows_of(lax.rem(x + k, XN))], cot_x.at[k - 1], x_peer(k))
        for k in range(1, XN)
    ]

    scaling = gain[...].astype(F32)
    load_own.wait()
    own_float = own_in[...].astype(F32)
    mixed[:own_rows] = (own_float * scaling).astype(BF16)
    column = jnp.sum(own_float * own_float, axis=1, keepdims=True)
    own_sum[...] = jnp.broadcast_to(to_row(column, own_rows), own_sum.shape)
    own_copies = [
        copies.start(own_sum, own_sums.at[k - 1], m_peer(k)) for k in range(1, widths)
    ]

    value = cot_parts[rows_of(x)].astype(F32)
    for k, copy in enumerate(cot_copies):
        copy.wait_recv()
        value = value + cot_x[k].astype(F32)
    cot_sum[...] = value.astype(BF16)
    cot_copies = [copies.start(cot_sum, cot_z.at[k - 1], z_peer(k)) for k in range(1, ZN)]

    total = own_sum[...]
    for k, copy in enumerate(own_copies):
        copy.wait_recv()
        total = total + own_sums[k]
    factor = lax.rsqrt(total / width_total + EPS)
    keeper = (replica != failed[section]).astype(F32)
    column = to_column(factor[:1], own_rows) * keeper
    back[:own_rows] = (own_cotangent[...].astype(F32) * column).astype(BF16)

    source = lax.rem(failed[upcoming], XN)
    load_p.wait()
    far_p.wait_recv()
    cand_p[2] = jnp.where(source == lax.rem(x + 3, XN), cand_p[1], cand_p[0])
    pass_p = copies.start(cand_p.at[2], cand_a.at[2], x_peer(1))
    load_n.wait()
    far_n.wait_recv()
    cand_n[2] = jnp.where(source == lax.rem(x + 1, XN), cand_n[1], cand_n[0])
    pass_n = copies.start(cand_n.at[2], cand_b.at[2], x_peer(3))

    value = cot_sum[...].astype(F32)
    for k, copy in enumerate(cot_copies):
        copy.wait_recv()
        value = value + cot_z[k].astype(F32)
    cot_all[m] = value.astype(BF16)
    cot_copies = [
        copies.start(cot_all.at[m], cot_all.at[m], m_peer(k)) for k in range(1, widths)
    ]

    here = source == x
    load_a.wait()
    near_a.wait_recv()
    pass_p.wait_recv()
    one = jnp.where(source == lax.rem(x + 1, XN), cand_a[1], cand_a[2])
    chosen[0] = jnp.where(here, cand_a[0], one)
    ahead = [copies.start(chosen.at[0], arrived.at[0], {"pipe": upcoming})]
    load_b.wait()
    near_b.wait_recv()
    pass_n.wait_recv()
    one = jnp.where(source == lax.rem(x + 3, XN), cand_b[1], cand_b[2])
    chosen[1] = jnp.where(here, cand_b[0], one)
    ahead += [copies.start(chosen.at[1], arrived.at[1], {"pipe": upcoming})]

    for copy in cot_copies:
        copy.wait_recv()
    load_w.wait()

    valid = (failed[section] // XN == z).astype(F32)
    masked = scaling * valid
    columns = []
    for part in range(2):
        ahead[part].wait_recv()
        rows = slice(own_rows + part * half, own_rows + (part + 1) * half)
        value = arrived[part].astype(F32)
        mixed[rows] = (value * masked).astype(BF16)
        columns.append(jnp.sum(value * value, axis=1, keepdims=True))
    padded = replay_sum.shape[1]
    row = to_row(jnp.concatenate(columns, axis=0), padded)
    replay_sum[...] = jnp.broadcast_to(row, replay_sum.shape)
    sum_copies = [
        copies.start(replay_sum, replay_sums.at[k - 1], m_peer(k)) for k in range(1, widths)
    ]
    partial = jnp.dot(mixed[own_rows:], weight_in[...], preferred_element_type=F32)
    for place in range(widths):
        key_parts[place] = partial[:, place * share : (place + 1) * share].astype(BF16)
    key_copies = [
        copies.start(key_parts.at[lax.rem(m + k, widths)], key_got.at[k - 1], m_peer(k))
        for k in range(1, widths)
    ]

    total = replay_sum[...]
    for k, copy in enumerate(sum_copies):
        copy.wait_recv()
        total = total + replay_sums[k]
    factor = lax.rsqrt(total / width_total + EPS)
    column = to_column(factor[:1], chunk)
    for place in range(widths):
        value = cot_all[place].astype(F32) * column
        back[own_rows:, place * share : (place + 1) * share] = value.astype(BF16)

    contract = (((0,), (0,)), ((), ()))
    group = XN * block
    grad_copies = []
    for step in range(ZN):
        place = lax.rem(z + 1 + step, ZN)
        window = pl.ds(pl.multiple_of(place * group, 128), group)
        product = lax.dot_general(
            mixed[:, window], back[...], contract, preferred_element_type=F32
        ).astype(BF16)
        for k in range(XN):
            grad_parts[step, k] = product[k * block : (k + 1) * block]
        grad_copies.append(
            [
                copies.start(
                    grad_parts.at[step, lax.rem(x + k, XN)], grad_x.at[step, k - 1], x_peer(k)
                )
                for k in range(1, XN)
            ]
        )

    value = key_parts[m].astype(F32)
    for k, copy in enumerate(key_copies):
        copy.wait_recv()
        value = value + key_got[k].astype(F32)
    key_all[rows_of(x)] = (value * column).astype(BF16)
    key_copies = [
        copies.start(key_all.at[rows_of(x)], key_all.at[rows_of(x)], x_peer(k))
        for k in range(1, XN)
    ]

    last = []
    for step in range(ZN):
        value = grad_parts[step, x].astype(F32)
        for k, copy in enumerate(grad_copies[step]):
            copy.wait_recv()
            value = value + grad_x[step, k].astype(F32)
        if step < ZN - 1:
            grad_half[step] = value.astype(BF16)
            last.append(copies.start(grad_half.at[step], grad_z.at[step], z_peer(step + 1)))
        else:
            grad_out[...] = value
        if step == 0:
            for copy in key_copies:
                copy.wait_recv()
            key_last_copies = []
            for k in range(ZN):
                there = lax.rem(z + k, ZN) * XN + x
                for j in range(slot_total):
                    named = table[section, 2 * there + j]
                    kept = counts[section, there] > j
                    value = None
                    for batch in range(batches):
                        rows = slice(batch * token_total, (batch + 1) * token_total)
                        hit = jnp.logical_and(named == batch, kept).astype(F32)
                        term = key_all[rows].astype(F32) * hit
                        value = term if value is None else value + term
                    key_pick[k, j * token_total : (j + 1) * token_total] = value.astype(BF16)
                if k > 0:
                    key_last_copies.append(
                        copies.start(key_pick.at[k], key_z.at[k - 1], z_peer(k))
                    )

    value = key_pick[0].astype(F32)
    for k, copy in enumerate(key_last_copies):
        copy.wait_recv()
        value = value + key_z[k].astype(F32)
    key_last[...] = value.astype(BF16)
    final = copies.start(key_last, key_in, {"pipe": upcoming})

    value = grad_out[...]
    for k, copy in enumerate(last):
        copy.wait_recv()
        value = value + grad_z[k].astype(F32)
    grad_out[...] = value
    final.wait_recv()
    keys_out[...] = key_in[...]
    copies.finish()


def per_device(
    stash, own_input, gain, key_weight, own_cotangent, replay_cotangent, failed, counts, table
):
    widths = lax.axis_size("mp")
    batches, tokens, features = stash.shape[2:]
    half = batches * tokens // (2 * XN)
    chunk = 2 * half
    own_rows = own_input.shape[2]
    key_width = key_weight.shape[2]
    share = key_width // widths
    slots = replay_cotangent.shape[2]
    replay_rows = slots * tokens
    block = features // (XN * ZN)
    others = max(widths - 1, 1)
    padded = -(-chunk // 128) * 128
    remote = 4 + 3 + 3 + 3 + 3 * (widths - 1) + 2 + (widths - 1) + 4 * 3 + 3 + 3 + 3 + 1 + 2
    vmem = pl.BlockSpec(memory_space=pltpu.VMEM)
    smem = pl.BlockSpec(memory_space=pltpu.SMEM)
    whole = pl.BlockSpec(memory_space=pl.ANY)
    keys, gradient = pl.pallas_call(
        functools.partial(kernel, features * widths),
        out_shape=(
            jax.ShapeDtypeStruct((replay_rows, share), BF16),
            jax.ShapeDtypeStruct((block, key_width), F32),
        ),
        in_specs=[smem, smem, smem, whole, whole, vmem, whole, vmem, vmem],
        out_specs=(vmem, vmem),
        scratch_shapes=[
            pltpu.VMEM((3, half, features), BF16),
            pltpu.VMEM((3, half, features), BF16),
            pltpu.VMEM((3, half, features), BF16),
            pltpu.VMEM((3, half, features), BF16),
            pltpu.VMEM((2, half, features), BF16),
            pltpu.VMEM((2, half, features), BF16),
            pltpu.VMEM((own_rows, features), BF16),
            pltpu.VMEM((features, key_width), BF16),
            pltpu.VMEM((4 * chunk, share), BF16),
            pltpu.VMEM((XN - 1, chunk, share), BF16),
            pltpu.VMEM((chunk, share), BF16),
            pltpu.VMEM((ZN - 1, chunk, share), BF16),
            pltpu.VMEM((widths, chunk, share), BF16),
            pltpu.VMEM((8, own_rows), F32),
            pltpu.VMEM((others, 8, own_rows), F32),
            pltpu.VMEM((8, padded), F32),
            pltpu.VMEM((others, 8, padded), F32),
            pltpu.VMEM((own_rows + chunk, features), BF16),
            pltpu.VMEM((own_rows + chunk, key_width), BF16),
            pltpu.VMEM((widths, chunk, share), BF16),
            pltpu.VMEM((others, chunk, share), BF16),
            pltpu.VMEM((4 * chunk, share), BF16),
            pltpu.VMEM((ZN, replay_rows, share), BF16),
            pltpu.VMEM((ZN - 1, replay_rows, share), BF16),
            pltpu.VMEM((replay_rows, share), BF16),
            pltpu.VMEM((replay_rows, share), BF16),
            pltpu.VMEM((ZN, XN, block, key_width), BF16),
            pltpu.VMEM((ZN, XN - 1, block, key_width), BF16),
            pltpu.VMEM((ZN - 1, block, key_width), BF16),
            pltpu.VMEM((ZN - 1, block, key_width), BF16),
            pltpu.SemaphoreType.DMA((6,)),
            pltpu.SemaphoreType.DMA((remote,)),
            pltpu.SemaphoreType.DMA((remote,)),
        ],
        compiler_params=pltpu.CompilerParams(
            collective_id=0, has_side_effects=True, vmem_limit_bytes=48 * 1024 * 1024
        ),
    )(
        failed,
        counts,
        table.reshape(table.shape[0], -1),
        stash.reshape(2 * XN, half, features),
        own_input.reshape(own_rows, features),
        gain,
        key_weight.reshape(features, key_width),
        own_cotangent.reshape(own_rows, key_width),
        replay_cotangent.reshape(replay_rows, key_width),
    )
    return (keys.reshape(1, 1, slots, tokens, share), gradient[None])


def solution(mesh):
    in_specs = (
        P("pipe", "dp", None, None, "mp"),
        P("pipe", "dp", None, "mp"),
        P("pipe", "mp"),
        P("pipe", "mp", None),
        P("pipe", "dp", None, None),
        P("pipe", "dp", None, None, None),
        P(),
        P(),
        P(),
    )
    out_specs = (P("pipe", "dp", None, None, "mp"), P("pipe", ("mp", "dp"), None))
    return jax.shard_map(
        per_device, mesh=mesh, in_specs=in_specs, out_specs=out_specs, check_vma=False
    )
```

```python
import functools
import jax
import jax.numpy as jnp
from jax import lax
from jax.experimental import pallas as pl
from jax.experimental.pallas import tpu as pltpu
from jax.sharding import PartitionSpec as P

MESH = pl.DeviceIdType.MESH
XN = 4
ZN = 4
PIECES = 2
EPS = 1e-05
F32 = jnp.float32
BF16 = jnp.bfloat16


def diagonal(rows, columns):
    return lax.broadcasted_iota(jnp.int32, (rows, columns), 0) == lax.broadcasted_iota(
        jnp.int32, (rows, columns), 1
    )


def to_row(column, columns):
    rows = column.shape[0]
    return jnp.sum(jnp.where(diagonal(rows, columns), column, 0.0), axis=0, keepdims=True)


def to_column(row, rows):
    return jnp.sum(jnp.where(diagonal(rows, row.shape[1]), row, 0.0), axis=1, keepdims=True)


class Copies:
    def __init__(self, send, recv):
        self.send, self.recv, self.count, self.started = send, recv, 0, []

    def start(self, source, target, device):
        copy = pltpu.make_async_remote_copy(
            src_ref=source,
            dst_ref=target,
            send_sem=self.send.at[self.count],
            recv_sem=self.recv.at[self.count],
            device_id=device,
            device_id_type=MESH,
        )
        self.count += 1
        copy.start()
        self.started.append(copy)
        return copy

    def finish(self):
        for copy in self.started:
            copy.wait_send()


def kernel(
    width_total,
    failed_hbm,
    counts_hbm,
    table_hbm,
    stash,
    own_input,
    gain_hbm,
    weight,
    own_cotangent,
    replay_cotangent,
    keys_out,
    grad_out,
    failed,
    counts,
    table,
    gain,
    own_cot,
    replay_cot,
    cand_p,
    cand_n,
    cand_a,
    cand_b,
    chosen,
    arrived,
    own_in,
    weight_in,
    cot_parts,
    cot_x,
    cot_sum,
    cot_z,
    cot_all,
    own_sum,
    own_sums,
    replay_sum,
    replay_sums,
    mixed,
    back,
    key_parts,
    key_got,
    key_all,
    key_pick,
    key_z,
    key_last,
    key_in,
    grad_parts,
    grad_far,
    grad_pass,
    grad_x,
    half_far,
    half_got,
    half_send,
    half_z,
    local_sem,
    send_sem,
    recv_sem,
):
    section = lax.axis_index("pipe")
    replica = lax.axis_index("dp")
    m = lax.axis_index("mp")
    sections = lax.axis_size("pipe")
    widths = lax.axis_size("mp")
    x = lax.rem(replica, XN)
    z = replica // XN
    half, features = stash.shape[1:]
    chunk = 2 * half
    own_rows = own_input.shape[0]
    key_width = weight.shape[1]
    share = key_width // widths
    block = features // (XN * ZN)
    upcoming = lax.rem(section + 1, sections)
    previous = lax.rem(section + sections - 1, sections)

    def x_peer(k):
        return {"dp": z * XN + lax.rem(x + k, XN)}

    def z_peer(k):
        return {"dp": lax.rem(z + k, ZN) * XN + x}

    def m_peer(k):
        return {"mp": lax.rem(m + k, widths)}

    barrier = pltpu.get_barrier_semaphore()
    peers = [x_peer(k) for k in range(1, XN)]
    peers += [z_peer(k) for k in range(1, ZN)]
    peers += [m_peer(k) for k in range(1, widths)]
    peers += [{"pipe": upcoming}, {"pipe": previous}]
    for peer in peers:
        pl.semaphore_signal(barrier, inc=1, device_id=peer, device_id_type=MESH)

    loads = []

    def load(source, target):
        copy = pltpu.make_async_copy(source, target, local_sem.at[len(loads)])
        copy.start()
        loads.append(copy)
        return copy

    load_counts = load(counts_hbm, counts)
    load_table = load(table_hbm, table)
    load_failed = load(failed_hbm, failed)
    load_replay = load(replay_cotangent, replay_cot)
    load_gain = load(gain_hbm, gain)
    load_own = load(own_input, own_in)
    load_cot = load(own_cotangent, own_cot)
    load_p = load(stash.at[2 * lax.rem(x + 1, XN)], cand_p.at[0])
    load_n = load(stash.at[2 * lax.rem(x + 3, XN) + 1], cand_n.at[0])
    load_a = load(stash.at[2 * x], cand_a.at[0])
    load_b = load(stash.at[2 * x + 1], cand_b.at[0])
    load_w = load(weight, weight_in)

    quarter = pl.ds(pl.multiple_of(m * share, 128), share)
    slot_total = 2
    token_total = replay_cotangent.shape[0] // slot_total
    batches = 4 * chunk // token_total
    load_counts.wait()
    load_table.wait()
    load_replay.wait()
    live = counts[section, replica]
    cot = replay_cot[:, quarter].astype(F32)
    for batch in range(batches):
        value = None
        for j in range(slot_total):
            hit = jnp.logical_and(table[section, j, replica] == batch, live > j)
            term = cot[j * token_total : (j + 1) * token_total] * hit.astype(F32)
            value = term if value is None else value + term
        cot_parts[batch * token_total : (batch + 1) * token_total] = value.astype(BF16)

    def rows_of(place):
        return pl.ds(pl.multiple_of(place * chunk, 16), chunk)

    pl.semaphore_wait(barrier, len(peers))
    copies = Copies(send_sem, recv_sem)
    cot_copies = [
        copies.start(cot_parts.at[rows_of(lax.rem(x + k, XN))], cot_x.at[k - 1], x_peer(k))
        for k in range(1, XN)
    ]

    far = 2 * lax.rem(x + 2, XN)
    windows = [slice(c * features // PIECES, (c + 1) * features // PIECES) for c in range(PIECES)]
    far_p, far_n, near_a, near_b = [], [], [], []
    for w in windows:
        far_p.append(copies.start(stash.at[far, :, w], cand_p.at[1, :, w], x_peer(1)))
        far_n.append(copies.start(stash.at[far + 1, :, w], cand_n.at[1, :, w], x_peer(3)))
        near = 2 * lax.rem(x + 1, XN) + 1
        near_b.append(copies.start(stash.at[near, :, w], cand_b.at[1, :, w], x_peer(1)))
        near = 2 * lax.rem(x + 3, XN)
        near_a.append(copies.start(stash.at[near, :, w], cand_a.at[1, :, w], x_peer(3)))

    load_gain.wait()
    scaling = gain[...].astype(F32)
    load_own.wait()
    own_float = own_in[...].astype(F32)
    mixed[:own_rows] = (own_float * scaling).astype(BF16)
    column = jnp.sum(own_float * own_float, axis=1, keepdims=True)
    own_sum[...] = jnp.broadcast_to(to_row(column, own_rows), own_sum.shape)
    own_copies = [
        copies.start(own_sum, own_sums.at[k - 1], m_peer(k)) for k in range(1, widths)
    ]

    value = cot_parts[rows_of(x)].astype(F32)
    for k, copy in enumerate(cot_copies):
        copy.wait_recv()
        value = value + cot_x[k].astype(F32)
    cot_sum[...] = value.astype(BF16)
    cot_copies = [copies.start(cot_sum, cot_z.at[k - 1], z_peer(k)) for k in range(1, ZN)]

    total = own_sum[...]
    for k, copy in enumerate(own_copies):
        copy.wait_recv()
        total = total + own_sums[k]
    factor = lax.rsqrt(total / width_total + EPS)
    load_failed.wait()
    load_cot.wait()
    keeper = (replica != failed[section]).astype(F32)
    column = to_column(factor[:1], own_rows) * keeper
    back[:own_rows] = (own_cot[...].astype(F32) * column).astype(BF16)

    source = lax.rem(failed[upcoming], XN)
    here = source == x
    before = source == lax.rem(x + 3, XN)
    after = source == lax.rem(x + 1, XN)
    load_p.wait()
    load_n.wait()
    pass_p, pass_n = [], []

    def relay(c):
        w = windows[c]
        far_p[c].wait_recv()
        cand_p[2, :, w] = jnp.where(before, cand_p[1, :, w], cand_p[0, :, w])
        pass_p.append(copies.start(cand_p.at[2, :, w], cand_a.at[2, :, w], x_peer(1)))
        far_n[c].wait_recv()
        cand_n[2, :, w] = jnp.where(after, cand_n[1, :, w], cand_n[0, :, w])
        pass_n.append(copies.start(cand_n.at[2, :, w], cand_b.at[2, :, w], x_peer(3)))

    ahead = []

    def choose(c):
        w = windows[c]
        near_a[c].wait_recv()
        pass_p[c].wait_recv()
        one = jnp.where(after, cand_a[1, :, w], cand_a[2, :, w])
        chosen[0, :, w] = jnp.where(here, cand_a[0, :, w], one)
        ahead.append(copies.start(chosen.at[0, :, w], arrived.at[0, :, w], {"pipe": upcoming}))
        near_b[c].wait_recv()
        pass_n[c].wait_recv()
        one = jnp.where(before, cand_b[1, :, w], cand_b[2, :, w])
        chosen[1, :, w] = jnp.where(here, cand_b[0, :, w], one)
        ahead.append(copies.start(chosen.at[1, :, w], arrived.at[1, :, w], {"pipe": upcoming}))

    relay(0)
    value = cot_sum[...].astype(F32)
    for k, copy in enumerate(cot_copies):
        copy.wait_recv()
        value = value + cot_z[k].astype(F32)
    cot_all[m] = value.astype(BF16)
    cot_copies = [
        copies.start(cot_all.at[m], cot_all.at[m], m_peer(k)) for k in range(1, widths)
    ]
    load_a.wait()
    load_b.wait()
    for c in range(1, PIECES):
        relay(c)
        choose(c - 1)

    valid = (failed[section] // XN == z).astype(F32)
    masked = scaling * valid
    columns = [0.0, 0.0]

    def take(c):
        w = windows[c]
        for part in range(2):
            ahead[2 * c + part].wait_recv()
            rows = slice(own_rows + part * half, own_rows + (part + 1) * half)
            value = arrived[part, :, w].astype(F32)
            mixed[rows, w] = (value * masked[:, w]).astype(BF16)
            columns[part] = columns[part] + jnp.sum(value * value, axis=1, keepdims=True)

    choose(PIECES - 1)
    load_w.wait()
    for c in range(PIECES):
        take(c)
    padded = replay_sum.shape[1]
    row = to_row(jnp.concatenate(columns, axis=0), padded)
    replay_sum[...] = jnp.broadcast_to(row, replay_sum.shape)
    sum_copies = [
        copies.start(replay_sum, replay_sums.at[k - 1], m_peer(k)) for k in range(1, widths)
    ]
    partial = jnp.dot(mixed[own_rows:], weight_in[...], preferred_element_type=F32)
    for place in range(widths):
        key_parts[place] = partial[:, place * share : (place + 1) * share].astype(BF16)
    key_copies = [
        copies.start(key_parts.at[lax.rem(m + k, widths)], key_got.at[k - 1], m_peer(k))
        for k in range(1, widths)
    ]

    for copy in cot_copies:
        copy.wait_recv()
    total = replay_sum[...]
    for k, copy in enumerate(sum_copies):
        copy.wait_recv()
        total = total + replay_sums[k]
    factor = lax.rsqrt(total / width_total + EPS)
    column = to_column(factor[:1], chunk)
    for place in range(widths):
        value = cot_all[place].astype(F32) * column
        back[own_rows:, place * share : (place + 1) * share] = value.astype(BF16)

    contract = (((0,), (0,)), ((), ()))
    group = XN * block
    middle = block // 2
    first, second = slice(0, middle), slice(middle, block)
    turns = (2, 1, 3, 0)
    straight, passing, added = [], [], []

    def issue(step):
        place = lax.rem(z + turns[step], ZN)
        window = pl.ds(pl.multiple_of(place * group, 128), group)
        product = lax.dot_general(
            mixed[:, window], back[...], contract, preferred_element_type=F32
        ).astype(BF16)
        for k in range(XN):
            grad_parts[step, k] = product[k * block : (k + 1) * block]
        parts = grad_parts.at[step]
        over = parts.at[lax.rem(x + 2, XN)]
        passing.append(
            (
                copies.start(over.at[first], grad_far.at[step, 0], x_peer(1)),
                copies.start(over.at[second], grad_far.at[step, 1], x_peer(3)),
            )
        )
        right, left = parts.at[lax.rem(x + 1, XN)], parts.at[lax.rem(x + 3, XN)]
        straight.append(
            (
                copies.start(right.at[second], grad_x.at[step, 0, second], x_peer(1)),
                copies.start(left.at[first], grad_x.at[step, 1, first], x_peer(3)),
            )
        )

    def pass_on(step):
        to_p, to_n = passing[step]
        to_p.wait_recv()
        value = grad_parts[step, lax.rem(x + 1, XN), first].astype(F32)
        grad_pass[step, 0] = (value + grad_far[step, 0].astype(F32)).astype(BF16)
        sent_p = copies.start(grad_pass.at[step, 0], grad_x.at[step, 0, first], x_peer(1))
        to_n.wait_recv()
        value = grad_parts[step, lax.rem(x + 3, XN), second].astype(F32)
        grad_pass[step, 1] = (value + grad_far[step, 1].astype(F32)).astype(BF16)
        sent_n = copies.start(grad_pass.at[step, 1], grad_x.at[step, 1, second], x_peer(3))
        added.append((sent_p, sent_n))

    def summed(step):
        for copy in straight[step] + added[step]:
            copy.wait_recv()
        value = grad_parts[step, x].astype(F32)
        return value + grad_x[step, 0].astype(F32) + grad_x[step, 1].astype(F32)

    issue(0)
    value = key_parts[m].astype(F32)
    for k, copy in enumerate(key_copies):
        copy.wait_recv()
        value = value + key_got[k].astype(F32)
    key_all[rows_of(x)] = (value * column).astype(BF16)
    key_copies = [
        copies.start(key_all.at[rows_of(x)], key_all.at[rows_of(x)], x_peer(k))
        for k in range(1, XN)
    ]
    issue(1)
    pass_on(0)
    issue(2)

    for copy in key_copies:
        copy.wait_recv()
    key_copies = []
    for k in range(ZN):
        there = lax.rem(z + k, ZN) * XN + x
        for j in range(slot_total):
            named = table[section, j, there]
            kept = counts[section, there] > j
            value = None
            for batch in range(batches):
                rows = slice(batch * token_total, (batch + 1) * token_total)
                hit = jnp.logical_and(named == batch, kept).astype(F32)
                term = key_all[rows].astype(F32) * hit
                value = term if value is None else value + term
            key_pick[k, j * token_total : (j + 1) * token_total] = value.astype(BF16)
        if k > 0:
            key_copies.append(copies.start(key_pick.at[k], key_z.at[k - 1], z_peer(k)))

    value = summed(0)
    half_far[...] = value.astype(BF16)
    over_p = copies.start(half_far.at[first], half_got.at[0], z_peer(1))
    over_n = copies.start(half_far.at[second], half_got.at[1], z_peer(3))
    pass_on(1)
    issue(3)
    arriving = []

    value = summed(1)
    half_send[0, second] = value[middle:].astype(BF16)
    arriving.append(
        copies.start(half_send.at[0, second], half_z.at[0, second], z_peer(1))
    )
    pass_on(2)
    over_p.wait_recv()
    half_send[0, first] = (value[:middle] + half_got[0].astype(F32)).astype(BF16)
    arriving.append(copies.start(half_send.at[0, first], half_z.at[0, first], z_peer(1)))

    value = summed(2)
    half_send[1, first] = value[:middle].astype(BF16)
    arriving.append(copies.start(half_send.at[1, first], half_z.at[1, first], z_peer(3)))
    over_n.wait_recv()
    half_send[1, second] = (value[middle:] + half_got[1].astype(F32)).astype(BF16)
    arriving.append(
        copies.start(half_send.at[1, second], half_z.at[1, second], z_peer(3))
    )

    pass_on(3)
    value = key_pick[0].astype(F32)
    for k, copy in enumerate(key_copies):
        copy.wait_recv()
        value = value + key_z[k].astype(F32)
    key_last[...] = value.astype(BF16)
    final = copies.start(key_last, key_in, {"pipe": upcoming})

    value = summed(3)
    for copy in arriving:
        copy.wait_recv()
    grad_out[...] = value + half_z[0].astype(F32) + half_z[1].astype(F32)
    final.wait_recv()
    keys_out[...] = key_in[...]
    copies.finish()


def per_device(
    stash, own_input, gain, key_weight, own_cotangent, replay_cotangent, failed, counts, table
):
    widths = lax.axis_size("mp")
    batches, tokens, features = stash.shape[2:]
    half = batches * tokens // (2 * XN)
    chunk = 2 * half
    own_rows = own_input.shape[2]
    key_width = key_weight.shape[2]
    share = key_width // widths
    slots = replay_cotangent.shape[2]
    replay_rows = slots * tokens
    block = features // (XN * ZN)
    others = max(widths - 1, 1)
    padded = -(-chunk // 128) * 128
    remote = 8 * PIECES + 3 + 3 + 4 * (widths - 1) + 6 * ZN + 3 + 3 + 6 + 1
    vmem = pl.BlockSpec(memory_space=pltpu.VMEM)
    whole = pl.BlockSpec(memory_space=pltpu.HBM)
    keys, gradient = pl.pallas_call(
        functools.partial(kernel, features * widths),
        out_shape=(
            jax.ShapeDtypeStruct((replay_rows, share), BF16),
            jax.ShapeDtypeStruct((block, key_width), F32),
        ),
        in_specs=[whole] * 9,
        out_specs=(vmem, vmem),
        scratch_shapes=[
            pltpu.SMEM(failed.shape, jnp.int32),
            pltpu.SMEM(counts.shape, jnp.int32),
            pltpu.SMEM((table.shape[0], slots, table.shape[1]), jnp.int32),
            pltpu.VMEM((1, features), BF16),
            pltpu.VMEM((own_rows, key_width), BF16),
            pltpu.VMEM((replay_rows, key_width), BF16),
            pltpu.VMEM((3, half, features), BF16),
            pltpu.VMEM((3, half, features), BF16),
            pltpu.VMEM((3, half, features), BF16),
            pltpu.VMEM((3, half, features), BF16),
            pltpu.VMEM((2, half, features), BF16),
            pltpu.VMEM((2, half, features), BF16),
            pltpu.VMEM((own_rows, features), BF16),
            pltpu.VMEM((features, key_width), BF16),
            pltpu.VMEM((4 * chunk, share), BF16),
            pltpu.VMEM((XN - 1, chunk, share), BF16),
            pltpu.VMEM((chunk, share), BF16),
            pltpu.VMEM((ZN - 1, chunk, share), BF16),
            pltpu.VMEM((widths, chunk, share), BF16),
            pltpu.VMEM((8, own_rows), F32),
            pltpu.VMEM((others, 8, own_rows), F32),
            pltpu.VMEM((8, padded), F32),
            pltpu.VMEM((others, 8, padded), F32),
            pltpu.VMEM((own_rows + chunk, features), BF16),
            pltpu.VMEM((own_rows + chunk, key_width), BF16),
            pltpu.VMEM((widths, chunk, share), BF16),
            pltpu.VMEM((others, chunk, share), BF16),
            pltpu.VMEM((4 * chunk, share), BF16),
            pltpu.VMEM((ZN, replay_rows, share), BF16),
            pltpu.VMEM((ZN - 1, replay_rows, share), BF16),
            pltpu.VMEM((replay_rows, share), BF16),
            pltpu.VMEM((replay_rows, share), BF16),
            pltpu.VMEM((ZN, XN, block, key_width), BF16),
            pltpu.VMEM((ZN, 2, block // 2, key_width), BF16),
            pltpu.VMEM((ZN, 2, block // 2, key_width), BF16),
            pltpu.VMEM((ZN, 2, block, key_width), BF16),
            pltpu.VMEM((block, key_width), BF16),
            pltpu.VMEM((2, block // 2, key_width), BF16),
            pltpu.VMEM((2, block, key_width), BF16),
            pltpu.VMEM((2, block, key_width), BF16),
            pltpu.SemaphoreType.DMA((12,)),
            pltpu.SemaphoreType.DMA((remote,)),
            pltpu.SemaphoreType.DMA((remote,)),
        ],
        compiler_params=pltpu.CompilerParams(
            collective_id=0, has_side_effects=True, vmem_limit_bytes=63 * 1024 * 1024
        ),
    )(
        failed,
        counts,
        jnp.swapaxes(table, 1, 2),
        stash.reshape(2 * XN, half, features),
        own_input.reshape(own_rows, features),
        gain,
        key_weight.reshape(features, key_width),
        own_cotangent.reshape(own_rows, key_width),
        replay_cotangent.reshape(replay_rows, key_width),
    )
    return (keys.reshape(1, 1, slots, tokens, share), gradient[None])


def solution(mesh):
    in_specs = (
        P("pipe", "dp", None, None, "mp"),
        P("pipe", "dp", None, "mp"),
        P("pipe", "mp"),
        P("pipe", "mp", None),
        P("pipe", "dp", None, None),
        P("pipe", "dp", None, None, None),
        P(),
        P(),
        P(),
    )
    out_specs = (P("pipe", "dp", None, None, "mp"), P("pipe", ("mp", "dp"), None))
    return jax.shard_map(
        per_device, mesh=mesh, in_specs=in_specs, out_specs=out_specs, check_vma=False
    )
```

```python
import functools
import jax
import jax.numpy as jnp
from jax import lax
from jax.experimental import pallas as pl
from jax.experimental.pallas import tpu as pltpu
from jax.sharding import PartitionSpec as P

MESH = pl.DeviceIdType.MESH
XN = 4
ZN = 4
PIECES = ZN
TURNS = (2, 1, 3, 0)
EPS = 1e-05
F32 = jnp.float32
BF16 = jnp.bfloat16


def diagonal(rows, columns):
    return lax.broadcasted_iota(jnp.int32, (rows, columns), 0) == lax.broadcasted_iota(
        jnp.int32, (rows, columns), 1
    )


def to_row(column, columns):
    rows = column.shape[0]
    return jnp.sum(jnp.where(diagonal(rows, columns), column, 0.0), axis=0, keepdims=True)


def to_column(row, rows):
    return jnp.sum(jnp.where(diagonal(rows, row.shape[1]), row, 0.0), axis=1, keepdims=True)


class Copies:
    def __init__(self, send, recv):
        self.send, self.recv, self.count, self.started = send, recv, 0, []

    def start(self, source, target, device):
        copy = pltpu.make_async_remote_copy(
            src_ref=source,
            dst_ref=target,
            send_sem=self.send.at[self.count],
            recv_sem=self.recv.at[self.count],
            device_id=device,
            device_id_type=MESH,
        )
        self.count += 1
        copy.start()
        self.started.append(copy)
        return copy

    def finish(self):
        for copy in self.started:
            copy.wait_send()


def kernel(
    width_total,
    failed_hbm,
    counts_hbm,
    table_hbm,
    stash,
    own_input,
    gain_hbm,
    weight,
    own_cotangent,
    replay_cotangent,
    keys_out,
    grad_out,
    failed,
    counts,
    table,
    gain,
    own_cot,
    replay_cot,
    cand_p,
    cand_n,
    cand_a,
    cand_b,
    chosen,
    arrived,
    own_in,
    weight_in,
    cot_parts,
    cot_x,
    cot_sum,
    cot_z,
    cot_all,
    own_sum,
    own_sums,
    held,
    replay_sum,
    replay_sums,
    square_total,
    square_x,
    square_sent,
    square_got,
    mixed,
    back,
    key_total,
    key_parts,
    key_got,
    key_all,
    key_pick,
    key_z,
    key_last,
    key_in,
    grad_parts,
    grad_far,
    grad_pass,
    grad_x,
    half_far,
    half_got,
    half_send,
    half_z,
    local_sem,
    send_sem,
    recv_sem,
):
    section = lax.axis_index("pipe")
    replica = lax.axis_index("dp")
    m = lax.axis_index("mp")
    sections = lax.axis_size("pipe")
    widths = lax.axis_size("mp")
    x = lax.rem(replica, XN)
    z = replica // XN
    half, features = stash.shape[1:]
    chunk = 2 * half
    own_rows = own_input.shape[0]
    key_width = weight.shape[1]
    share = key_width // widths
    block = features // (XN * ZN)
    upcoming = lax.rem(section + 1, sections)
    previous = lax.rem(section + sections - 1, sections)

    def x_peer(k):
        return {"dp": z * XN + lax.rem(x + k, XN)}

    def z_peer(k):
        return {"dp": lax.rem(z + k, ZN) * XN + x}

    def m_peer(k):
        return {"mp": lax.rem(m + k, widths)}

    barrier = pltpu.get_barrier_semaphore()
    peers = [x_peer(k) for k in range(1, XN)]
    peers += [z_peer(k) for k in range(1, ZN)]
    peers += [m_peer(k) for k in range(1, widths)]
    peers += [{"pipe": upcoming}, {"pipe": previous}]
    for peer in peers:
        pl.semaphore_signal(barrier, inc=1, device_id=peer, device_id_type=MESH)

    loads = []

    def load(source, target):
        copy = pltpu.make_async_copy(source, target, local_sem.at[len(loads)])
        copy.start()
        loads.append(copy)
        return copy

    load_counts = load(counts_hbm, counts)
    load_table = load(table_hbm, table)
    load_failed = load(failed_hbm, failed)
    load_replay = load(replay_cotangent, replay_cot)
    load_gain = load(gain_hbm, gain)
    load_own = load(own_input, own_in)
    load_cot = load(own_cotangent, own_cot)
    load_held = load(stash, held)
    load_w = load(weight, weight_in)

    quarter = pl.ds(pl.multiple_of(m * share, 128), share)
    slot_total = 2
    token_total = replay_cotangent.shape[0] // slot_total
    batches = 4 * chunk // token_total
    load_counts.wait()
    load_table.wait()
    load_replay.wait()
    live = counts[section, replica]
    cot = replay_cot[:, quarter].astype(F32)
    for batch in range(batches):
        value = None
        for j in range(slot_total):
            hit = jnp.logical_and(table[section, j, replica] == batch, live > j)
            term = cot[j * token_total : (j + 1) * token_total] * hit.astype(F32)
            value = term if value is None else value + term
        cot_parts[batch * token_total : (batch + 1) * token_total] = value.astype(BF16)

    def rows_of(place):
        return pl.ds(pl.multiple_of(place * chunk, 16), chunk)

    pl.semaphore_wait(barrier, len(peers))
    copies = Copies(send_sem, recv_sem)
    cot_copies = [
        copies.start(cot_parts.at[rows_of(lax.rem(x + k, XN))], cot_x.at[k - 1], x_peer(k))
        for k in range(1, XN)
    ]

    group = XN * block
    windows = [
        pl.ds(pl.multiple_of(lax.rem(z + turn, ZN) * group, 128), group) for turn in TURNS
    ]
    right, over, left = (lax.rem(x + k, XN) for k in range(1, XN))
    far_p, far_n, near_a, near_b = [], [], [], []

    def bulk(c):
        w = windows[c]
        far_p.append(copies.start(stash.at[2 * over, :, w], cand_p.at[0, :, w], x_peer(1)))
        far_n.append(copies.start(stash.at[2 * over + 1, :, w], cand_n.at[0, :, w], x_peer(3)))
        near_b.append(copies.start(stash.at[2 * right + 1, :, w], cand_b.at[0, :, w], x_peer(1)))
        near_a.append(copies.start(stash.at[2 * left, :, w], cand_a.at[0, :, w], x_peer(3)))

    bulk(0)
    bulk(1)

    load_gain.wait()
    load_own.wait()
    own_float = own_in[...].astype(F32)
    mixed[:own_rows] = (own_float * gain[...].astype(F32)).astype(BF16)
    column = jnp.sum(own_float * own_float, axis=1, keepdims=True)
    own_sum[...] = jnp.broadcast_to(to_row(column, own_rows), own_sum.shape)
    own_copies = [
        copies.start(own_sum, own_sums.at[k - 1], m_peer(k)) for k in range(1, widths)
    ]
    load_held.wait()
    padded = replay_sum.shape[1]
    for part in range(2 * XN):
        value = held[part].astype(F32)
        column = jnp.sum(value * value, axis=1, keepdims=True)
        replay_sum[part : part + 1] = to_row(column, padded)
    sum_copies = [
        copies.start(replay_sum, replay_sums.at[k - 1], m_peer(k)) for k in range(1, widths)
    ]

    load_failed.wait()
    source = lax.rem(failed[upcoming], XN)
    here = source == x
    before = source == left
    after = source == right
    pass_p, pass_n, ahead = [], [], []

    def relay(c):
        w = windows[c]
        far_p[c].wait_recv()
        cand_p[1, :, w] = jnp.where(before, cand_p[0, :, w], held[2 * right, :, w])
        pass_p.append(copies.start(cand_p.at[1, :, w], cand_a.at[1, :, w], x_peer(1)))
        far_n[c].wait_recv()
        cand_n[1, :, w] = jnp.where(after, cand_n[0, :, w], held[2 * left + 1, :, w])
        pass_n.append(copies.start(cand_n.at[1, :, w], cand_b.at[1, :, w], x_peer(3)))

    def choose(c):
        w = windows[c]
        near_a[c].wait_recv()
        pass_p[c].wait_recv()
        one = jnp.where(after, cand_a[0, :, w], cand_a[1, :, w])
        chosen[0, :, w] = jnp.where(here, held[2 * x, :, w], one)
        ahead.append(copies.start(chosen.at[0, :, w], arrived.at[0, :, w], {"pipe": upcoming}))
        near_b[c].wait_recv()
        pass_n[c].wait_recv()
        one = jnp.where(before, cand_b[0, :, w], cand_b[1, :, w])
        chosen[1, :, w] = jnp.where(here, held[2 * x + 1, :, w], one)
        ahead.append(copies.start(chosen.at[1, :, w], arrived.at[1, :, w], {"pipe": upcoming}))

    value = cot_parts[rows_of(x)].astype(F32)
    for k, copy in enumerate(cot_copies):
        copy.wait_recv()
        value = value + cot_x[k].astype(F32)
    cot_sum[...] = value.astype(BF16)
    cot_copies = [copies.start(cot_sum, cot_z.at[k - 1], z_peer(k)) for k in range(1, ZN)]

    total = replay_sum[...]
    for k, copy in enumerate(sum_copies):
        copy.wait_recv()
        total = total + replay_sums[k]
    square_total[...] = total
    square_copies = [copies.start(square_total, square_x.at[k - 1], x_peer(k)) for k in range(1, XN)]

    relay(0)
    bulk(2)

    total = own_sum[...]
    for k, copy in enumerate(own_copies):
        copy.wait_recv()
        total = total + own_sums[k]
    factor = lax.rsqrt(total / width_total + EPS)
    load_cot.wait()
    keeper = (replica != failed[section]).astype(F32)
    column = to_column(factor[:1], own_rows) * keeper
    back[:own_rows] = (own_cot[...].astype(F32) * column).astype(BF16)

    relay(1)
    bulk(3)

    value = square_total[...]
    for k, copy in enumerate(square_copies):
        copy.wait_recv()
        value = jnp.where(source == lax.rem(x + XN - 1 - k, XN), square_x[k], value)
    square_sent[...] = value
    square_ahead = copies.start(square_sent, square_got, {"pipe": upcoming})
    choose(0)

    value = cot_sum[...].astype(F32)
    for k, copy in enumerate(cot_copies):
        copy.wait_recv()
        value = value + cot_z[k].astype(F32)
    cot_all[m] = value.astype(BF16)
    cot_copies = [
        copies.start(cot_all.at[m], cot_all.at[m], m_peer(k)) for k in range(1, widths)
    ]

    relay(2)
    choose(1)
    relay(3)
    choose(2)

    valid = (failed[section] // XN == z).astype(F32)
    load_w.wait()

    def take(c):
        w = windows[c]
        masked = gain[:, w].astype(F32) * valid
        for part in range(2):
            ahead[2 * c + part].wait_recv()
            rows = slice(own_rows + part * half, own_rows + (part + 1) * half)
            mixed[rows, w] = (arrived[part, :, w].astype(F32) * masked).astype(BF16)
        term = jnp.dot(mixed[own_rows:, w], weight_in[w], preferred_element_type=F32)
        key_total[...] = term if c == 0 else key_total[...] + term

    contract = (((0,), (0,)), ((), ()))
    middle = block // 2
    first, second = slice(0, middle), slice(middle, block)
    straight, passing, added = [], [], []

    def issue(step):
        window = windows[step]
        product = lax.dot_general(
            mixed[:, window], back[...], contract, preferred_element_type=F32
        ).astype(BF16)
        for k in range(XN):
            grad_parts[step, k] = product[k * block : (k + 1) * block]
        parts = grad_parts.at[step]
        distant = parts.at[over]
        passing.append(
            (
                copies.start(distant.at[first], grad_far.at[step, 0], x_peer(1)),
                copies.start(distant.at[second], grad_far.at[step, 1], x_peer(3)),
            )
        )
        straight.append(
            (
                copies.start(parts.at[right, second], grad_x.at[step, 0, second], x_peer(1)),
                copies.start(parts.at[left, first], grad_x.at[step, 1, first], x_peer(3)),
            )
        )

    def pass_on(step):
        to_p, to_n = passing[step]
        to_p.wait_recv()
        value = grad_parts[step, lax.rem(x + 1, XN), first].astype(F32)
        grad_pass[step, 0] = (value + grad_far[step, 0].astype(F32)).astype(BF16)
        sent_p = copies.start(grad_pass.at[step, 0], grad_x.at[step, 0, first], x_peer(1))
        to_n.wait_recv()
        value = grad_parts[step, lax.rem(x + 3, XN), second].astype(F32)
        grad_pass[step, 1] = (value + grad_far[step, 1].astype(F32)).astype(BF16)
        sent_n = copies.start(grad_pass.at[step, 1], grad_x.at[step, 1, second], x_peer(3))
        added.append((sent_p, sent_n))

    def summed(step):
        for copy in straight[step] + added[step]:
            copy.wait_recv()
        value = grad_parts[step, x].astype(F32)
        return value + grad_x[step, 0].astype(F32) + grad_x[step, 1].astype(F32)

    take(0)
    for copy in cot_copies:
        copy.wait_recv()
    square_ahead.wait_recv()
    columns = []
    for part in range(2):
        factor = lax.rsqrt(square_got[pl.ds(2 * x + part, 1)] / width_total + EPS)
        columns.append(to_column(factor, half))
    column = jnp.concatenate(columns, axis=0)
    for place in range(widths):
        value = cot_all[place].astype(F32) * column
        back[own_rows:, place * share : (place + 1) * share] = value.astype(BF16)
    issue(0)
    take(1)
    issue(1)
    choose(3)
    pass_on(0)
    take(2)
    issue(2)
    take(3)

    for place in range(widths):
        key_parts[place] = key_total[:, place * share : (place + 1) * share].astype(BF16)
    key_copies = [
        copies.start(key_parts.at[lax.rem(m + k, widths)], key_got.at[k - 1], m_peer(k))
        for k in range(1, widths)
    ]
    pass_on(1)

    value = summed(0)
    half_far[...] = value.astype(BF16)
    over_p = copies.start(half_far.at[first], half_got.at[0], z_peer(1))
    over_n = copies.start(half_far.at[second], half_got.at[1], z_peer(3))
    value = key_parts[m].astype(F32)
    for k, copy in enumerate(key_copies):
        copy.wait_recv()
        value = value + key_got[k].astype(F32)
    key_all[rows_of(x)] = (value * column).astype(BF16)
    key_copies = [
        copies.start(key_all.at[rows_of(x)], key_all.at[rows_of(x)], x_peer(k))
        for k in range(1, XN)
    ]
    issue(3)
    arriving = []

    value = summed(1)
    half_send[0, second] = value[middle:].astype(BF16)
    arriving.append(
        copies.start(half_send.at[0, second], half_z.at[0, second], z_peer(1))
    )
    pass_on(2)
    over_p.wait_recv()
    half_send[0, first] = (value[:middle] + half_got[0].astype(F32)).astype(BF16)
    arriving.append(copies.start(half_send.at[0, first], half_z.at[0, first], z_peer(1)))

    for copy in key_copies:
        copy.wait_recv()
    key_copies = []
    for k in range(ZN):
        there = lax.rem(z + k, ZN) * XN + x
        for j in range(slot_total):
            named = table[section, j, there]
            kept = counts[section, there] > j
            value = None
            for batch in range(batches):
                rows = slice(batch * token_total, (batch + 1) * token_total)
                hit = jnp.logical_and(named == batch, kept).astype(F32)
                term = key_all[rows].astype(F32) * hit
                value = term if value is None else value + term
            key_pick[k, j * token_total : (j + 1) * token_total] = value.astype(BF16)
        if k > 0:
            key_copies.append(copies.start(key_pick.at[k], key_z.at[k - 1], z_peer(k)))

    value = summed(2)
    half_send[1, first] = value[:middle].astype(BF16)
    arriving.append(copies.start(half_send.at[1, first], half_z.at[1, first], z_peer(3)))
    over_n.wait_recv()
    half_send[1, second] = (value[middle:] + half_got[1].astype(F32)).astype(BF16)
    arriving.append(
        copies.start(half_send.at[1, second], half_z.at[1, second], z_peer(3))
    )

    pass_on(3)
    value = key_pick[0].astype(F32)
    for k, copy in enumerate(key_copies):
        copy.wait_recv()
        value = value + key_z[k].astype(F32)
    key_last[...] = value.astype(BF16)
    final = copies.start(key_last, key_in, {"pipe": upcoming})

    value = summed(3)
    for copy in arriving:
        copy.wait_recv()
    grad_out[...] = value + half_z[0].astype(F32) + half_z[1].astype(F32)
    final.wait_recv()
    keys_out[...] = key_in[...]
    copies.finish()


def per_device(
    stash, own_input, gain, key_weight, own_cotangent, replay_cotangent, failed, counts, table
):
    widths = lax.axis_size("mp")
    batches, tokens, features = stash.shape[2:]
    half = batches * tokens // (2 * XN)
    chunk = 2 * half
    own_rows = own_input.shape[2]
    key_width = key_weight.shape[2]
    share = key_width // widths
    slots = replay_cotangent.shape[2]
    replay_rows = slots * tokens
    block = features // (XN * ZN)
    others = max(widths - 1, 1)
    padded = -(-half // 128) * 128
    remote = 8 * PIECES + 4 * (widths - 1) + 6 * ZN + 3 + 3 + 3 + 1 + 3 + 3 + 1 + 6
    vmem = pl.BlockSpec(memory_space=pltpu.VMEM)
    whole = pl.BlockSpec(memory_space=pltpu.HBM)
    keys, gradient = pl.pallas_call(
        functools.partial(kernel, features * widths),
        out_shape=(
            jax.ShapeDtypeStruct((replay_rows, share), BF16),
            jax.ShapeDtypeStruct((block, key_width), F32),
        ),
        in_specs=[whole] * 9,
        out_specs=(vmem, vmem),
        scratch_shapes=[
            pltpu.SMEM(failed.shape, jnp.int32),
            pltpu.SMEM(counts.shape, jnp.int32),
            pltpu.SMEM((table.shape[0], slots, table.shape[1]), jnp.int32),
            pltpu.VMEM((1, features), BF16),
            pltpu.VMEM((own_rows, key_width), BF16),
            pltpu.VMEM((replay_rows, key_width), BF16),
            pltpu.VMEM((2, half, features), BF16),
            pltpu.VMEM((2, half, features), BF16),
            pltpu.VMEM((2, half, features), BF16),
            pltpu.VMEM((2, half, features), BF16),
            pltpu.VMEM((2, half, features), BF16),
            pltpu.VMEM((2, half, features), BF16),
            pltpu.VMEM((own_rows, features), BF16),
            pltpu.VMEM((features, key_width), BF16),
            pltpu.VMEM((4 * chunk, share), BF16),
            pltpu.VMEM((XN - 1, chunk, share), BF16),
            pltpu.VMEM((chunk, share), BF16),
            pltpu.VMEM((ZN - 1, chunk, share), BF16),
            pltpu.VMEM((widths, chunk, share), BF16),
            pltpu.VMEM((8, own_rows), F32),
            pltpu.VMEM((others, 8, own_rows), F32),
            pltpu.VMEM((2 * XN, half, features), BF16),
            pltpu.VMEM((2 * XN, padded), F32),
            pltpu.VMEM((others, 2 * XN, padded), F32),
            pltpu.VMEM((2 * XN, padded), F32),
            pltpu.VMEM((XN - 1, 2 * XN, padded), F32),
            pltpu.VMEM((2 * XN, padded), F32),
            pltpu.VMEM((2 * XN, padded), F32),
            pltpu.VMEM((own_rows + chunk, features), BF16),
            pltpu.VMEM((own_rows + chunk, key_width), BF16),
            pltpu.VMEM((chunk, key_width), F32),
            pltpu.VMEM((widths, chunk, share), BF16),
            pltpu.VMEM((others, chunk, share), BF16),
            pltpu.VMEM((4 * chunk, share), BF16),
            pltpu.VMEM((ZN, replay_rows, share), BF16),
            pltpu.VMEM((ZN - 1, replay_rows, share), BF16),
            pltpu.VMEM((replay_rows, share), BF16),
            pltpu.VMEM((replay_rows, share), BF16),
            pltpu.VMEM((ZN, XN, block, key_width), BF16),
            pltpu.VMEM((ZN, 2, block // 2, key_width), BF16),
            pltpu.VMEM((ZN, 2, block // 2, key_width), BF16),
            pltpu.VMEM((ZN, 2, block, key_width), BF16),
            pltpu.VMEM((block, key_width), BF16),
            pltpu.VMEM((2, block // 2, key_width), BF16),
            pltpu.VMEM((2, block, key_width), BF16),
            pltpu.VMEM((2, block, key_width), BF16),
            pltpu.SemaphoreType.DMA((9,)),
            pltpu.SemaphoreType.DMA((remote,)),
            pltpu.SemaphoreType.DMA((remote,)),
        ],
        compiler_params=pltpu.CompilerParams(
            collective_id=0, has_side_effects=True, vmem_limit_bytes=63 * 1024 * 1024
        ),
    )(
        failed,
        counts,
        jnp.swapaxes(table, 1, 2),
        stash.reshape(2 * XN, half, features),
        own_input.reshape(own_rows, features),
        gain,
        key_weight.reshape(features, key_width),
        own_cotangent.reshape(own_rows, key_width),
        replay_cotangent.reshape(replay_rows, key_width),
    )
    return (keys.reshape(1, 1, slots, tokens, share), gradient[None])


def solution(mesh):
    in_specs = (
        P("pipe", "dp", None, None, "mp"),
        P("pipe", "dp", None, "mp"),
        P("pipe", "mp"),
        P("pipe", "mp", None),
        P("pipe", "dp", None, None),
        P("pipe", "dp", None, None, None),
        P(),
        P(),
        P(),
    )
    out_specs = (P("pipe", "dp", None, None, "mp"), P("pipe", ("mp", "dp"), None))
    return jax.shard_map(
        per_device, mesh=mesh, in_specs=in_specs, out_specs=out_specs, check_vma=False
    )
```

```python
import functools
import jax
import jax.numpy as jnp
from jax import lax
from jax.experimental import pallas as pl
from jax.experimental.pallas import tpu as pltpu
from jax.sharding import PartitionSpec as P

MESH = pl.DeviceIdType.MESH
XN = 4
ZN = 4
PIECES = ZN
TURNS = (2, 1, 3, 0)
EPS = 1e-05
F32 = jnp.float32
BF16 = jnp.bfloat16


def diagonal(rows, columns):
    return lax.broadcasted_iota(jnp.int32, (rows, columns), 0) == lax.broadcasted_iota(
        jnp.int32, (rows, columns), 1
    )


def to_row(column, columns):
    rows = column.shape[0]
    return jnp.sum(jnp.where(diagonal(rows, columns), column, 0.0), axis=0, keepdims=True)


def to_column(row, rows):
    return jnp.sum(jnp.where(diagonal(rows, row.shape[1]), row, 0.0), axis=1, keepdims=True)


class Copies:
    def __init__(self, send, recv):
        self.send, self.recv, self.count, self.started = send, recv, 0, []

    def start(self, source, target, device):
        copy = pltpu.make_async_remote_copy(
            src_ref=source,
            dst_ref=target,
            send_sem=self.send.at[self.count],
            recv_sem=self.recv.at[self.count],
            device_id=device,
            device_id_type=MESH,
        )
        self.count += 1
        copy.start()
        self.started.append(copy)
        return copy

    def finish(self):
        for copy in self.started:
            copy.wait_send()


def kernel(
    width_total,
    failed_hbm,
    counts_hbm,
    table_hbm,
    stash,
    own_input,
    gain_hbm,
    weight,
    own_cotangent,
    replay_cotangent,
    keys_out,
    grad_out,
    failed,
    counts,
    table,
    gain,
    own_cot,
    replay_cot,
    cand_p,
    cand_n,
    cand_a,
    cand_b,
    chosen,
    arrived,
    own_in,
    weight_in,
    cot_parts,
    cot_x,
    cot_sum,
    cot_z,
    cot_all,
    own_sum,
    own_sums,
    held,
    replay_sum,
    replay_sums,
    square_total,
    square_x,
    square_sent,
    square_got,
    mixed,
    back,
    key_total,
    key_parts,
    key_got,
    key_all,
    key_pick,
    key_z,
    key_last,
    key_in,
    grad_parts,
    grad_far,
    grad_pass,
    grad_x,
    half_far,
    half_got,
    half_send,
    half_z,
    local_sem,
    send_sem,
    recv_sem,
):
    section = lax.axis_index("pipe")
    replica = lax.axis_index("dp")
    m = lax.axis_index("mp")
    sections = lax.axis_size("pipe")
    widths = lax.axis_size("mp")
    x = lax.rem(replica, XN)
    z = replica // XN
    half, features = stash.shape[1:]
    chunk = 2 * half
    own_rows = own_input.shape[0]
    key_width = weight.shape[1]
    share = key_width // widths
    block = features // (XN * ZN)
    upcoming = lax.rem(section + 1, sections)
    previous = lax.rem(section + sections - 1, sections)

    def x_peer(k):
        return {"dp": z * XN + lax.rem(x + k, XN)}

    def z_peer(k):
        return {"dp": lax.rem(z + k, ZN) * XN + x}

    def m_peer(k):
        return {"mp": lax.rem(m + k, widths)}

    barrier = pltpu.get_barrier_semaphore()
    peers = [x_peer(k) for k in range(1, XN)]
    peers += [z_peer(k) for k in range(1, ZN)]
    peers += [m_peer(k) for k in range(1, widths)]
    peers += [{"pipe": upcoming}, {"pipe": previous}]
    for peer in peers:
        pl.semaphore_signal(barrier, inc=1, device_id=peer, device_id_type=MESH)

    loads = []

    def load(source, target):
        copy = pltpu.make_async_copy(source, target, local_sem.at[len(loads)])
        copy.start()
        loads.append(copy)
        return copy

    load_counts = load(counts_hbm, counts)
    load_table = load(table_hbm, table)
    load_failed = load(failed_hbm, failed)
    load_replay = load(replay_cotangent, replay_cot)
    load_gain = load(gain_hbm, gain)
    load_own = load(own_input, own_in)
    load_cot = load(own_cotangent, own_cot)
    load_held = load(stash, held)
    load_w = load(weight, weight_in)

    quarter = pl.ds(pl.multiple_of(m * share, 128), share)
    slot_total = 2
    token_total = replay_cotangent.shape[0] // slot_total
    batches = 4 * chunk // token_total
    load_counts.wait()
    load_table.wait()
    load_replay.wait()
    live = counts[section, replica]
    cot = replay_cot[:, quarter].astype(F32)
    for batch in range(batches):
        value = None
        for j in range(slot_total):
            hit = jnp.logical_and(table[section, j, replica] == batch, live > j)
            term = cot[j * token_total : (j + 1) * token_total] * hit.astype(F32)
            value = term if value is None else value + term
        cot_parts[batch * token_total : (batch + 1) * token_total] = value.astype(BF16)

    def rows_of(place):
        return pl.ds(pl.multiple_of(place * chunk, 16), chunk)

    pl.semaphore_wait(barrier, len(peers))
    copies = Copies(send_sem, recv_sem)
    cot_copies = [
        copies.start(cot_parts.at[rows_of(lax.rem(x + k, XN))], cot_x.at[k - 1], x_peer(k))
        for k in range(1, XN)
    ]

    group = XN * block
    windows = [
        pl.ds(pl.multiple_of(lax.rem(z + turn, ZN) * group, 128), group) for turn in TURNS
    ]
    right, over, left = (lax.rem(x + k, XN) for k in range(1, XN))
    far_p, far_n, near_a, near_b = [], [], [], []

    def bulk(c):
        w = windows[c]
        far_p.append(copies.start(stash.at[2 * over, :, w], cand_p.at[0, :, w], x_peer(1)))
        far_n.append(copies.start(stash.at[2 * over + 1, :, w], cand_n.at[0, :, w], x_peer(3)))
        near_b.append(copies.start(stash.at[2 * right + 1, :, w], cand_b.at[0, :, w], x_peer(1)))
        near_a.append(copies.start(stash.at[2 * left, :, w], cand_a.at[0, :, w], x_peer(3)))

    bulk(0)
    bulk(1)

    load_gain.wait()
    load_own.wait()
    own_float = own_in[...].astype(F32)
    mixed[:own_rows] = (own_float * gain[...].astype(F32)).astype(BF16)
    column = jnp.sum(own_float * own_float, axis=1, keepdims=True)
    own_sum[...] = jnp.broadcast_to(to_row(column, own_rows), own_sum.shape)
    own_copies = [
        copies.start(own_sum, own_sums.at[k - 1], m_peer(k)) for k in range(1, widths)
    ]
    load_held.wait()
    padded = replay_sum.shape[1]
    for part in range(2 * XN):
        value = held[part].astype(F32)
        column = jnp.sum(value * value, axis=1, keepdims=True)
        replay_sum[part : part + 1] = to_row(column, padded)
    sum_copies = [
        copies.start(replay_sum, replay_sums.at[k - 1], m_peer(k)) for k in range(1, widths)
    ]

    load_failed.wait()
    source = lax.rem(failed[upcoming], XN)
    here = source == x
    before = source == left
    after = source == right
    pass_p, pass_n, ahead = [], [], []

    def relay(c):
        w = windows[c]
        far_p[c].wait_recv()
        cand_p[1, :, w] = jnp.where(before, cand_p[0, :, w], held[2 * right, :, w])
        pass_p.append(copies.start(cand_p.at[1, :, w], cand_a.at[1, :, w], x_peer(1)))
        far_n[c].wait_recv()
        cand_n[1, :, w] = jnp.where(after, cand_n[0, :, w], held[2 * left + 1, :, w])
        pass_n.append(copies.start(cand_n.at[1, :, w], cand_b.at[1, :, w], x_peer(3)))

    def choose(c):
        w = windows[c]
        near_a[c].wait_recv()
        pass_p[c].wait_recv()
        one = jnp.where(after, cand_a[0, :, w], cand_a[1, :, w])
        chosen[0, :, w] = jnp.where(here, held[2 * x, :, w], one)
        ahead.append(copies.start(chosen.at[0, :, w], arrived.at[0, :, w], {"pipe": upcoming}))
        near_b[c].wait_recv()
        pass_n[c].wait_recv()
        one = jnp.where(before, cand_b[0, :, w], cand_b[1, :, w])
        chosen[1, :, w] = jnp.where(here, held[2 * x + 1, :, w], one)
        ahead.append(copies.start(chosen.at[1, :, w], arrived.at[1, :, w], {"pipe": upcoming}))

    value = cot_parts[rows_of(x)].astype(F32)
    for k, copy in enumerate(cot_copies):
        copy.wait_recv()
        value = value + cot_x[k].astype(F32)
    cot_sum[...] = value.astype(BF16)
    cot_copies = [copies.start(cot_sum, cot_z.at[k - 1], z_peer(k)) for k in range(1, ZN)]

    total = replay_sum[...]
    for k, copy in enumerate(sum_copies):
        copy.wait_recv()
        total = total + replay_sums[k]
    square_total[...] = total
    square_copies = [copies.start(square_total, square_x.at[k - 1], x_peer(k)) for k in range(1, XN)]

    relay(0)
    bulk(2)

    total = own_sum[...]
    for k, copy in enumerate(own_copies):
        copy.wait_recv()
        total = total + own_sums[k]
    factor = lax.rsqrt(total / width_total + EPS)
    load_cot.wait()
    keeper = (replica != failed[section]).astype(F32)
    column = to_column(factor[:1], own_rows) * keeper
    back[:own_rows] = (own_cot[...].astype(F32) * column).astype(BF16)

    relay(1)
    bulk(3)

    value = square_total[...]
    for k, copy in enumerate(square_copies):
        copy.wait_recv()
        value = jnp.where(source == lax.rem(x + XN - 1 - k, XN), square_x[k], value)
    square_sent[...] = value
    square_ahead = copies.start(square_sent, square_got, {"pipe": upcoming})
    choose(0)

    value = cot_sum[...].astype(F32)
    for k, copy in enumerate(cot_copies):
        copy.wait_recv()
        value = value + cot_z[k].astype(F32)
    cot_all[m] = value.astype(BF16)
    cot_copies = [
        copies.start(cot_all.at[m], cot_all.at[m], m_peer(k)) for k in range(1, widths)
    ]

    relay(2)
    choose(1)
    relay(3)
    choose(2)

    valid = (failed[section] // XN == z).astype(F32)
    load_w.wait()

    def take(c):
        w = windows[c]
        masked = gain[:, w].astype(F32) * valid
        for part in range(2):
            ahead[2 * c + part].wait_recv()
            rows = slice(own_rows + part * half, own_rows + (part + 1) * half)
            mixed[rows, w] = (arrived[part, :, w].astype(F32) * masked).astype(BF16)
        term = jnp.dot(mixed[own_rows:, w], weight_in[w], preferred_element_type=F32)
        key_total[...] = term if c == 0 else key_total[...] + term

    contract = (((0,), (0,)), ((), ()))
    middle = block // 2
    first, second = slice(0, middle), slice(middle, block)
    straight, passing, added = [], [], []

    def issue(step):
        window = windows[step]
        product = lax.dot_general(
            mixed[:, window], back[...], contract, preferred_element_type=F32
        ).astype(BF16)
        for k in range(XN):
            grad_parts[step, k] = product[k * block : (k + 1) * block]
        parts = grad_parts.at[step]
        distant = parts.at[over]
        passing.append(
            (
                copies.start(distant.at[first], grad_far.at[step, 0], x_peer(1)),
                copies.start(distant.at[second], grad_far.at[step, 1], x_peer(3)),
            )
        )
        straight.append(
            (
                copies.start(parts.at[right, second], grad_x.at[step, 0, second], x_peer(1)),
                copies.start(parts.at[left, first], grad_x.at[step, 1, first], x_peer(3)),
            )
        )

    def pass_on(step):
        to_p, to_n = passing[step]
        to_p.wait_recv()
        value = grad_parts[step, lax.rem(x + 1, XN), first].astype(F32)
        grad_pass[step, 0] = (value + grad_far[step, 0].astype(F32)).astype(BF16)
        sent_p = copies.start(grad_pass.at[step, 0], grad_x.at[step, 0, first], x_peer(1))
        to_n.wait_recv()
        value = grad_parts[step, lax.rem(x + 3, XN), second].astype(F32)
        grad_pass[step, 1] = (value + grad_far[step, 1].astype(F32)).astype(BF16)
        sent_n = copies.start(grad_pass.at[step, 1], grad_x.at[step, 1, second], x_peer(3))
        added.append((sent_p, sent_n))

    def summed(step):
        for copy in straight[step] + added[step]:
            copy.wait_recv()
        value = grad_parts[step, x].astype(F32)
        return value + grad_x[step, 0].astype(F32) + grad_x[step, 1].astype(F32)

    take(0)
    for copy in cot_copies:
        copy.wait_recv()
    square_ahead.wait_recv()
    columns = []
    for part in range(2):
        factor = lax.rsqrt(square_got[pl.ds(2 * x + part, 1)] / width_total + EPS)
        columns.append(to_column(factor, half))
    column = jnp.concatenate(columns, axis=0)
    for place in range(widths):
        value = cot_all[place].astype(F32) * column
        back[own_rows:, place * share : (place + 1) * share] = value.astype(BF16)
    issue(0)
    take(1)
    issue(1)
    choose(3)
    pass_on(0)
    take(2)
    issue(2)
    take(3)

    for place in range(widths):
        key_parts[place] = key_total[:, place * share : (place + 1) * share].astype(BF16)
    key_copies = [
        copies.start(key_parts.at[lax.rem(m + k, widths)], key_got.at[k - 1], m_peer(k))
        for k in range(1, widths)
    ]
    pass_on(1)
    issue(3)

    value = summed(0)
    half_far[...] = value.astype(BF16)
    over_p = copies.start(half_far.at[first], half_got.at[0], z_peer(1))
    over_n = copies.start(half_far.at[second], half_got.at[1], z_peer(3))
    value = key_parts[m].astype(F32)
    for k, copy in enumerate(key_copies):
        copy.wait_recv()
        value = value + key_got[k].astype(F32)
    key_all[rows_of(x)] = (value * column).astype(BF16)
    key_copies = [
        copies.start(key_all.at[rows_of(x)], key_all.at[rows_of(x)], x_peer(k))
        for k in range(1, XN)
    ]
    arriving = []

    pass_on(2)
    nearer = summed(1)
    half_send[0, second] = nearer[middle:].astype(BF16)
    arriving.append(
        copies.start(half_send.at[0, second], half_z.at[0, second], z_peer(1))
    )
    for copy in key_copies:
        copy.wait_recv()
    key_copies = []
    for k in range(ZN):
        there = lax.rem(z + k, ZN) * XN + x
        for j in range(slot_total):
            named = table[section, j, there]
            kept = counts[section, there] > j
            value = None
            for batch in range(batches):
                rows = slice(batch * token_total, (batch + 1) * token_total)
                hit = jnp.logical_and(named == batch, kept).astype(F32)
                term = key_all[rows].astype(F32) * hit
                value = term if value is None else value + term
            key_pick[k, j * token_total : (j + 1) * token_total] = value.astype(BF16)
        if k > 0:
            key_copies.append(copies.start(key_pick.at[k], key_z.at[k - 1], z_peer(k)))

    over_p.wait_recv()
    half_send[0, first] = (nearer[:middle] + half_got[0].astype(F32)).astype(BF16)
    arriving.append(copies.start(half_send.at[0, first], half_z.at[0, first], z_peer(1)))

    pass_on(3)
    value = summed(2)
    half_send[1, first] = value[:middle].astype(BF16)
    arriving.append(copies.start(half_send.at[1, first], half_z.at[1, first], z_peer(3)))
    over_n.wait_recv()
    half_send[1, second] = (value[middle:] + half_got[1].astype(F32)).astype(BF16)
    arriving.append(
        copies.start(half_send.at[1, second], half_z.at[1, second], z_peer(3))
    )

    value = key_pick[0].astype(F32)
    for k, copy in enumerate(key_copies):
        copy.wait_recv()
        value = value + key_z[k].astype(F32)
    key_last[...] = value.astype(BF16)
    final = copies.start(key_last, key_in, {"pipe": upcoming})

    value = summed(3)
    for copy in arriving:
        copy.wait_recv()
    grad_out[...] = value + half_z[0].astype(F32) + half_z[1].astype(F32)
    final.wait_recv()
    keys_out[...] = key_in[...]
    copies.finish()


def per_device(
    stash, own_input, gain, key_weight, own_cotangent, replay_cotangent, failed, counts, table
):
    widths = lax.axis_size("mp")
    batches, tokens, features = stash.shape[2:]
    half = batches * tokens // (2 * XN)
    chunk = 2 * half
    own_rows = own_input.shape[2]
    key_width = key_weight.shape[2]
    share = key_width // widths
    slots = replay_cotangent.shape[2]
    replay_rows = slots * tokens
    block = features // (XN * ZN)
    others = max(widths - 1, 1)
    padded = -(-half // 128) * 128
    remote = 8 * PIECES + 4 * (widths - 1) + 6 * ZN + 3 + 3 + 3 + 1 + 3 + 3 + 1 + 6
    vmem = pl.BlockSpec(memory_space=pltpu.VMEM)
    whole = pl.BlockSpec(memory_space=pltpu.HBM)
    keys, gradient = pl.pallas_call(
        functools.partial(kernel, features * widths),
        out_shape=(
            jax.ShapeDtypeStruct((replay_rows, share), BF16),
            jax.ShapeDtypeStruct((block, key_width), F32),
        ),
        in_specs=[whole] * 9,
        out_specs=(vmem, vmem),
        scratch_shapes=[
            pltpu.SMEM(failed.shape, jnp.int32),
            pltpu.SMEM(counts.shape, jnp.int32),
            pltpu.SMEM((table.shape[0], slots, table.shape[1]), jnp.int32),
            pltpu.VMEM((1, features), BF16),
            pltpu.VMEM((own_rows, key_width), BF16),
            pltpu.VMEM((replay_rows, key_width), BF16),
            pltpu.VMEM((2, half, features), BF16),
            pltpu.VMEM((2, half, features), BF16),
            pltpu.VMEM((2, half, features), BF16),
            pltpu.VMEM((2, half, features), BF16),
            pltpu.VMEM((2, half, features), BF16),
            pltpu.VMEM((2, half, features), BF16),
            pltpu.VMEM((own_rows, features), BF16),
            pltpu.VMEM((features, key_width), BF16),
            pltpu.VMEM((4 * chunk, share), BF16),
            pltpu.VMEM((XN - 1, chunk, share), BF16),
            pltpu.VMEM((chunk, share), BF16),
            pltpu.VMEM((ZN - 1, chunk, share), BF16),
            pltpu.VMEM((widths, chunk, share), BF16),
            pltpu.VMEM((8, own_rows), F32),
            pltpu.VMEM((others, 8, own_rows), F32),
            pltpu.VMEM((2 * XN, half, features), BF16),
            pltpu.VMEM((2 * XN, padded), F32),
            pltpu.VMEM((others, 2 * XN, padded), F32),
            pltpu.VMEM((2 * XN, padded), F32),
            pltpu.VMEM((XN - 1, 2 * XN, padded), F32),
            pltpu.VMEM((2 * XN, padded), F32),
            pltpu.VMEM((2 * XN, padded), F32),
            pltpu.VMEM((own_rows + chunk, features), BF16),
            pltpu.VMEM((own_rows + chunk, key_width), BF16),
            pltpu.VMEM((chunk, key_width), F32),
            pltpu.VMEM((widths, chunk, share), BF16),
            pltpu.VMEM((others, chunk, share), BF16),
            pltpu.VMEM((4 * chunk, share), BF16),
            pltpu.VMEM((ZN, replay_rows, share), BF16),
            pltpu.VMEM((ZN - 1, replay_rows, share), BF16),
            pltpu.VMEM((replay_rows, share), BF16),
            pltpu.VMEM((replay_rows, share), BF16),
            pltpu.VMEM((ZN, XN, block, key_width), BF16),
            pltpu.VMEM((ZN, 2, block // 2, key_width), BF16),
            pltpu.VMEM((ZN, 2, block // 2, key_width), BF16),
            pltpu.VMEM((ZN, 2, block, key_width), BF16),
            pltpu.VMEM((block, key_width), BF16),
            pltpu.VMEM((2, block // 2, key_width), BF16),
            pltpu.VMEM((2, block, key_width), BF16),
            pltpu.VMEM((2, block, key_width), BF16),
            pltpu.SemaphoreType.DMA((9,)),
            pltpu.SemaphoreType.DMA((remote,)),
            pltpu.SemaphoreType.DMA((remote,)),
        ],
        compiler_params=pltpu.CompilerParams(
            collective_id=0, has_side_effects=True, vmem_limit_bytes=63 * 1024 * 1024
        ),
    )(
        failed,
        counts,
        jnp.swapaxes(table, 1, 2),
        stash.reshape(2 * XN, half, features),
        own_input.reshape(own_rows, features),
        gain,
        key_weight.reshape(features, key_width),
        own_cotangent.reshape(own_rows, key_width),
        replay_cotangent.reshape(replay_rows, key_width),
    )
    return (keys.reshape(1, 1, slots, tokens, share), gradient[None])


def solution(mesh):
    in_specs = (
        P("pipe", "dp", None, None, "mp"),
        P("pipe", "dp", None, "mp"),
        P("pipe", "mp"),
        P("pipe", "mp", None),
        P("pipe", "dp", None, None),
        P("pipe", "dp", None, None, None),
        P(),
        P(),
        P(),
    )
    out_specs = (P("pipe", "dp", None, None, "mp"), P("pipe", ("mp", "dp"), None))
    return jax.shard_map(
        per_device, mesh=mesh, in_specs=in_specs, out_specs=out_specs, check_vma=False
    )
```
